32 devices in a mesh: seq: 8 (over y, x, core), head: 4 (over z).
Axes of the slice: x: 2, y: 2, z: 4, core: 2. Of those that a mesh axis runs over, the one named last changes fastest.
Arguments:
- queries: bfloat16 [4096, 64, 128], P('seq', 'head'), may hold values from -48 to 48
- keys_values: bfloat16 [4096, 2, 8, 128], P('seq'), may hold values from -6 to 6
- grad_out: bfloat16 [4096, 64, 128], P('seq', 'head'), may hold values from -6 to 6
- segments: int32 [4096], P('seq'), may hold values from 0 to 14, as said below
- partner: int32 [8], replicated, may hold values from 0 to 7, as said below
- prompt_blocks: int32 [8], replicated, may hold values from 1 to 4, as said below
Outputs:
- attention: bfloat16 [4096, 64, 128], P('seq', 'head')
- query_gradient: bfloat16 [4096, 64, 128], P('seq', 'head')
- kv_grad: bfloat16 [4096, 2048], P('seq', 'head')
The draws below stay inside these ranges and needn't reach their ends.
Inputs may be any that keep to these rules, and one draw needn't show every extreme that they name: `segments`: within each bin ids never fall; segment 0 begins at the bin's first token and holds more than 64 tokens; segment 1 follows it directly and is the bin's rejected response; the largest id is reached in some bin in every draw. partner[b] != b, every bin is the partner of exactly one bin, and following partner from any bin visits all bins. `prompt_blocks`: the largest value is reached in every draw.
All inputs are finite; a program needn't handle non-finite values.
Results may differ from the reference program's by a relative error of at most 0.025.
Values may be sent and summed in bfloat16 or wider, within the bound.
A program may use at most 128 MiB of HBM per device.

```python
import math
import jax
import jax.numpy as jnp
from jax import lax

HEADS = 64
KVH = 8
HD = 128
TOK_DEV = 512
PMAX = 64
BLK = 16
EXTRA_CUTS = 12
NBINS = 8
TOKENS = 4096
N_HEAD = 4


def paired_floats(key):
    query_key = jax.random.fold_in(key, 101)
    kv_key = jax.random.fold_in(key, 202)
    kv_values = jnp.clip(jax.random.normal(kv_key, (TOKENS, 2, KVH, HD), jnp.float32), -6.0, 6.0)
    query_values = jnp.clip(jax.random.normal(query_key, (TOKENS, HEADS, HD), jnp.float32), -6.0, 6.0)
    return (query_values, kv_values)


def draw_queries(key, part):
    query_values, kv_values = paired_floats(key)
    return query_values.astype(jnp.bfloat16)


def draw_keys_values(key, part):
    query_values, kv_values = paired_floats(key)
    return kv_values.astype(jnp.bfloat16)


def draw_segments(key, part):
    bin_keys = jax.random.split(jax.random.fold_in(key, 606), NBINS)
    full_spot = jax.random.randint(jax.random.fold_in(key, 616), (), 0, NBINS)
    full_flags = jnp.arange(NBINS) == full_spot

    def one_bin(bin_key, full_flag):
        first_key, second_key, start_key, dense_key, live_key = jax.random.split(bin_key, 5)
        first_cut = jax.random.randint(first_key, (), PMAX + 8, TOK_DEV // 2)
        second_cut = first_cut + jax.random.randint(second_key, (), 8, TOK_DEV // 4)
        starts = jax.random.randint(start_key, (EXTRA_CUTS,), 0, TOK_DEV)
        density = jnp.where(full_flag, 4, jax.random.randint(dense_key, (), 0, 4))
        live_cuts = jax.random.randint(live_key, (EXTRA_CUTS,), 0, 4) < density
        starts = jnp.where(live_cuts, jnp.maximum(starts, second_cut), TOK_DEV)
        cuts = jnp.concatenate([jnp.stack([first_cut, second_cut]), starts])
        places = jnp.arange(TOK_DEV)
        return jnp.sum((places[:, None] >= cuts[None, :]).astype(jnp.int32), axis=1)
    return jax.vmap(one_bin)(bin_keys, full_flags).reshape(TOKENS).astype(jnp.int32)


def draw_partner(key, part):
    ranks = jax.random.permutation(jax.random.fold_in(key, 707), NBINS).astype(jnp.int32)
    anchor = jax.random.randint(jax.random.fold_in(key, 717), (), 0, NBINS).astype(jnp.int32)
    half = NBINS // 2
    fixed = jnp.stack([anchor, anchor - 1, anchor - 1 + half, anchor + half]) % NBINS
    ranks = ranks.at[fixed].set(jnp.arange(4, dtype=jnp.int32) - 4)
    order = jnp.argsort(ranks, stable=True).astype(jnp.int32)
    following = jnp.roll(order, -1)
    return jnp.zeros((NBINS,), jnp.int32).at[order].set(following)


def draw_prompt_blocks(key, part):
    value_key = jax.random.fold_in(key, 808)
    spot_key = jax.random.fold_in(key, 909)
    values = jax.random.randint(value_key, (NBINS,), 1, PMAX // BLK + 1)
    spot = jax.random.randint(spot_key, (), 0, NBINS)
    return values.at[spot].set(PMAX // BLK).astype(jnp.int32)


def block_scale(own_key, dims, pieces, smallest, high):
    def one(dim, parts):
        draws = jax.random.uniform(jax.random.fold_in(jax.random.fold_in(own_key, 6), dim), (parts,), jnp.float32, smallest / len(pieces), high / len(pieces))
        return jnp.repeat(jnp.exp(draws), dims[dim] // parts).reshape((-1,) + (1,) * (len(dims) - dim - 1))

    level = one(*pieces[0])
    for cut in pieces[1:]:
        level = level * one(*cut)
    return level


def gaussian(key, shape, deviation, limit, cuts=(), kind=jnp.bfloat16):
    entries = deviation * jax.random.normal(key, shape, jnp.float32)
    if cuts:
        entries = entries * block_scale(key, shape, cuts, -0.22, 0.18)
    return jnp.clip(entries, -limit, limit).astype(kind)


def setup_inputs(seed: int = 0) -> dict:
    streams_of = jax.random.split(jax.random.key(seed), 7)
    return {
        "queries": draw_queries(jax.random.fold_in(streams_of[6], 71), 0),
        "keys_values": draw_keys_values(jax.random.fold_in(streams_of[6], 71), 0),
        "grad_out": gaussian(streams_of[2], (TOKENS, HEADS, HD), 1.0, 6.0, ((0, 8), (1, 4))),
        "segments": draw_segments(jax.random.fold_in(streams_of[6], 71), 0),
        "partner": draw_partner(jax.random.fold_in(streams_of[6], 71), 0),
        "prompt_blocks": draw_prompt_blocks(jax.random.fold_in(streams_of[6], 71), 0),
    }


def expanded_product(form, left, right):
    return jnp.einsum(form, left.astype(jnp.float32), right.astype(jnp.float32), precision=lax.Precision.HIGHEST)

def reference(queries, keys_values, grad_out, segments, partner, prompt_blocks):
    group_size = HEADS // KVH
    run_size = min(HEADS // N_HEAD, group_size)
    score_scaling = 1.0 / math.sqrt(HD)
    query_bins = queries.reshape(NBINS, TOK_DEV, KVH, group_size, HD)
    grad_bins = grad_out.reshape(NBINS, TOK_DEV, KVH, group_size, HD)
    kv_bins = keys_values.reshape(NBINS, TOK_DEV, 2, KVH, HD)
    seg_bins = segments.reshape(NBINS, TOK_DEV)
    prompt_bins = kv_bins[:, :PMAX]
    positions = jnp.arange(TOK_DEV, dtype=jnp.int32)
    prompt_places = jnp.arange(PMAX, dtype=jnp.int32)

    def run_sums(head_grads):
        rows_count = head_grads.shape[0]
        runs = head_grads.reshape(rows_count, KVH, group_size // run_size, run_size, HD)
        partial_sums = lax.optimization_barrier(jnp.sum(runs, axis=3)).astype(jnp.bfloat16)
        return lax.optimization_barrier(jnp.sum(partial_sums.astype(jnp.float32), axis=2))

    def one_bin(bin_index):
        owner_bin = partner[bin_index]
        query_tile = query_bins[bin_index]
        gradient_tile = grad_bins[bin_index]
        kv_block = kv_bins[bin_index]
        seg_block = seg_bins[bin_index]
        remote = prompt_bins[owner_bin]
        every_key_row = jnp.concatenate([kv_block[:, 0], remote[:, 0]], axis=0)
        every_value_row = jnp.concatenate([kv_block[:, 1], remote[:, 1]], axis=0)
        local_ok = (seg_block[:, None] == seg_block[None, :]) & (positions[None, :] <= positions[:, None])
        live_count = BLK * prompt_blocks[owner_bin]
        remote_ok = (seg_block[:, None] == 1) & (prompt_places[None, :] < live_count)
        allowed = jnp.concatenate([local_ok, remote_ok], axis=1)[None, None]
        score_matrix = expanded_product('imwh,lmh->mwil', query_tile, every_key_row) * score_scaling
        score_matrix = jnp.where(allowed, score_matrix, -jnp.inf)
        row_peak = lax.optimization_barrier(jnp.max(score_matrix, axis=-1, keepdims=True))
        weights_raw = jnp.where(allowed, jnp.exp(score_matrix - row_peak), jnp.float32(0.0))
        probabilities = weights_raw / lax.optimization_barrier(jnp.sum(weights_raw, axis=-1, keepdims=True))
        probability_lowprec = probabilities.astype(jnp.bfloat16)
        attention = expanded_product('aqiu,uax->iaqx', probability_lowprec, every_value_row).astype(jnp.bfloat16)
        row_delta = lax.optimization_barrier(jnp.sum(gradient_tile.astype(jnp.float32) * attention.astype(jnp.float32), axis=-1))
        row_delta = jnp.transpose(row_delta, (1, 2, 0))
        probability_gradient = expanded_product('imwh,lmh->mwil', gradient_tile, every_value_row)
        score_gradient = (probabilities * (probability_gradient - row_delta[..., None])).astype(jnp.bfloat16)
        query_gradient = (expanded_product('aqiu,uax->iaqx', score_gradient, every_key_row) * score_scaling).astype(jnp.bfloat16)
        key_head_rows = expanded_product('bjek,ebjz->kbjz', score_gradient, query_tile) * score_scaling
        value_head_rows = expanded_product('bjek,ebjz->kbjz', probability_lowprec, gradient_tile)
        stacked = jnp.stack([run_sums(key_head_rows), run_sums(value_head_rows)], axis=2)
        flat_grads = stacked.reshape(stacked.shape[0], 2 * KVH * HD)
        return (attention.reshape(TOK_DEV, HEADS, HD), query_gradient.reshape(TOK_DEV, HEADS, HD), flat_grads[:TOK_DEV], flat_grads[TOK_DEV:])
    attention, query_gradient, local_sums, remote_sums = lax.map(one_bin, jnp.arange(NBINS, dtype=jnp.int32))
    prompt_low = remote_sums.astype(jnp.bfloat16)
    source_of = jnp.zeros((NBINS,), jnp.int32).at[partner].set(jnp.arange(NBINS, dtype=jnp.int32))
    arrived = prompt_low[source_of].astype(jnp.float32)
    merged = local_sums.at[:, :PMAX].add(arrived)
    kv_grad = merged.astype(jnp.bfloat16).reshape(TOKENS, 2 * KVH * HD)
    return (attention.reshape(TOKENS, HEADS, HD), query_gradient.reshape(TOKENS, HEADS, HD), kv_grad)
```

```python
import functools
import math

import jax
import jax.numpy as jnp
from jax import lax
from jax.experimental import pallas as pl
from jax.experimental.pallas import tpu as pltpu
from jax.sharding import PartitionSpec as P

HEADS = 64
KVH = 8
PMAX = 64
BLK = 16
ROWS = 128
PAD = 128
MASKED = -1e30
LOG2E = math.log2(math.e)


def from_partner(value, axis, apart):
    mask = 2**apart
    pairs = [(source, source ^ mask) for source in range(lax.axis_size(axis))]
    return lax.ppermute(value, axis, pairs)


def slotted(parcel, wanted):
    mask = wanted.reshape((-1,) + (1,) * parcel.ndim)
    return jnp.where(mask, parcel[None], jnp.zeros((), parcel.dtype))


def head_total(block, sharing):
    flat = block.reshape(block.shape[0], -1)
    place = lax.axis_index("head")
    for bit in reversed(range(sharing.bit_length() - 1)):
        half = flat.shape[1] // 2
        mine = place // 2**bit % 2
        kept = lax.dynamic_slice_in_dim(flat, mine * half, half, 1)
        given = lax.dynamic_slice_in_dim(flat, (1 - mine) * half, half, 1)
        got = from_partner(given.astype(jnp.bfloat16), "head", bit).astype(given.dtype)
        flat = kept + got
    return flat


def dot(a, b):
    return jnp.dot(a, b, preferred_element_type=jnp.float32)


def dot_t(a, b):
    return lax.dot_general(a, b, (((1,), (1,)), ((), ())), preferred_element_type=jnp.float32)


def attend(
    heads, kvs, per_kv, chunks, scale,
    partner_ref, blocks_ref, q_ref, do_ref, kv_ref, seg_ref, got_ref,
    out_ref, dq_ref, own_ref, prompt_ref,
    qf, dof, af, dqf, kvf, kcat, vcat, segc, bias, dkt, dvt,
):
    chunk = pl.program_id(0)
    me = lax.axis_index("seq")
    rows = chunks * ROWS
    width = PAD + rows

    @pl.when(chunk == 0)
    def _():
        owner = partner_ref[me]
        kv_start = lax.axis_index("head") * heads // (HEADS // KVH)
        step = ROWS * 2 * KVH
        for part in range(chunks):
            kvf[part * step:(part + 1) * step, :] = kv_ref[part * step:(part + 1) * step, :].astype(jnp.float32)
        for g in range(kvs):
            k_rows = kvf[pl.ds(kv_start + g, rows, stride=2 * KVH), :]
            v_rows = kvf[pl.ds(kv_start + g + KVH, rows, stride=2 * KVH), :]
            kcat[g, PAD:, :] = k_rows.astype(jnp.bfloat16)
            vcat[g, PAD:, :128] = v_rows.astype(jnp.bfloat16)
            kcat[g, PMAX:PAD, :] = jnp.zeros((PAD - PMAX, 128), jnp.bfloat16)
            vcat[g, PMAX:PAD, :128] = jnp.zeros((PAD - PMAX, 128), jnp.bfloat16)
            kcat[g, :PMAX, :] = got_ref[owner, g * PMAX:(g + 1) * PMAX, :]
            vcat[g, :PMAX, :128] = got_ref[owner, (kvs + g) * PMAX:(kvs + g + 1) * PMAX, :]
            vcat[g, :, 128:] = jnp.ones((width, 128), jnp.bfloat16)
        segc[...] = jnp.broadcast_to(seg_ref[...].astype(jnp.float32), (128, rows)).T
        dkt[...] = jnp.zeros_like(dkt)
        dvt[...] = jnp.zeros_like(dvt)

    qf[...] = q_ref[...].astype(jnp.float32)
    dof[...] = do_ref[...].astype(jnp.float32)

    def work(c):
        wide = PAD + (c + 1) * ROWS
        live = BLK * blocks_ref[partner_ref[me]]
        column = segc[c * ROWS:(c + 1) * ROWS, :]
        place = lax.broadcasted_iota(jnp.int32, (ROWS, 128), 1)
        row = lax.broadcasted_iota(jnp.int32, (ROWS, 128), 0)
        bias[:, :PAD] = jnp.where((column == 1.0) & (place < live), 0.0, MASKED)
        for j in range(c + 1):
            same = column == seg_ref[:, j * ROWS:(j + 1) * ROWS].astype(jnp.float32)
            if j == c:
                same = same & (place <= row)
            bias[:, PAD + j * ROWS:PAD + (j + 1) * ROWS] = jnp.where(same, 0.0, MASKED)

        def pair(i, carry):
            h = 2 * i
            g = h // per_kv
            first, second = pl.ds(h, ROWS, stride=heads), pl.ds(h + 1, ROWS, stride=heads)
            q32 = jnp.concatenate([qf[first, :], qf[second, :]], axis=0)
            q = q32.astype(jnp.bfloat16)
            k = kcat[g, :wide, :]
            s = dot_t(q, k) * (scale * LOG2E)
            b = bias[:, :wide]
            t = s + jnp.concatenate([b, b], axis=0)
            p = jnp.exp2(t - jnp.max(t, axis=1, keepdims=True))
            pb = p.astype(jnp.bfloat16)
            mixed = dot(pb, vcat[g, :wide, :])
            inverse = 1.0 / mixed[:, 128:]
            attention = (mixed[:, :128] * inverse).astype(jnp.bfloat16).astype(jnp.float32)
            af[first, :] = attention[:ROWS]
            af[second, :] = attention[ROWS:]
            do = jnp.concatenate([dof[first, :], dof[second, :]], axis=0)
            dos = (do * inverse).astype(jnp.bfloat16)
            dos32 = dos.astype(jnp.float32)
            delta = jnp.sum(dos32 * attention, axis=1, keepdims=True)
            dp = dot_t(dos, vcat[g, :wide, :128])
            ds = (p * (dp - delta)).astype(jnp.bfloat16)
            dq = dot(ds, k) * scale
            dqf[first, :] = dq[:ROWS]
            dqf[second, :] = dq[ROWS:]
            dkt[g, :, :wide] += dot(q32.T.astype(jnp.bfloat16), ds)
            dvt[g, :, :wide] += dot(dos32.T.astype(jnp.bfloat16), pb)
            return carry

        lax.fori_loop(0, heads // 2, pair, 0, unroll=2)

    for c in range(chunks):
        pl.when(chunk == c)(functools.partial(work, c))
    out_ref[...] = af[...].astype(jnp.bfloat16)
    dq_ref[...] = dqf[...].astype(jnp.bfloat16)

    @pl.when(chunk == chunks - 1)
    def _():
        for g in range(kvs):
            for part, grads in ((0, dkt[g] * scale), (1, dvt[g])):
                turned = grads.T.astype(jnp.bfloat16)
                at = (2 * g + part) * 128
                own_ref[:, at:at + 128] = turned[PAD:]
                prompt_ref[:, at:at + 128] = turned[:PMAX]


def body(queries, keys_values, grad_out, segments, partner, prompt_blocks):
    rows_here, heads_here, head_dim = queries.shape
    group_size = HEADS // KVH
    kv_here = max(1, heads_here // group_size)
    per_kv = heads_here // kv_here
    sharing = max(1, group_size // heads_here)
    kv_start = lax.axis_index("head") * heads_here // group_size
    self_index = lax.axis_index("seq")
    bin_count = lax.axis_size("seq")
    chunks = rows_here // ROWS
    width = PAD + rows_here
    bin_ids = jnp.arange(bin_count, dtype=jnp.int32)
    owner_bin = partner[self_index]
    source = jnp.sum(jnp.where(partner == self_index, bin_ids, 0))
    prompt = lax.dynamic_slice_in_dim(keys_values[:PMAX], kv_start, kv_here, 2)
    parcel = jnp.transpose(prompt, (1, 2, 0, 3)).reshape(2 * kv_here * PMAX, head_dim)
    received = lax.all_to_all(
        slotted(parcel, partner == self_index), "seq", split_axis=0, concat_axis=0, tiled=True
    )
    block = pl.BlockSpec((ROWS * heads_here, head_dim), lambda c: (c, 0))
    whole = pl.BlockSpec(memory_space=pltpu.VMEM)
    flat = jax.ShapeDtypeStruct((rows_here * heads_here, head_dim), jnp.bfloat16)
    f32, bf16 = jnp.float32, jnp.bfloat16
    attention, query_gradient, own, prompt_grad = pl.pallas_call(
        functools.partial(attend, heads_here, kv_here, per_kv, chunks, 1.0 / math.sqrt(head_dim)),
        grid=(chunks,),
        in_specs=[pl.BlockSpec(memory_space=pltpu.SMEM)] * 2 + [block, block, whole, whole, whole],
        out_specs=[block, block, whole, whole],
        out_shape=[
            flat,
            flat,
            jax.ShapeDtypeStruct((rows_here, kv_here * 2 * head_dim), bf16),
            jax.ShapeDtypeStruct((PMAX, kv_here * 2 * head_dim), bf16),
        ],
        scratch_shapes=[pltpu.VMEM((ROWS * heads_here, head_dim), f32)] * 4
        + [
            pltpu.VMEM((rows_here * 2 * KVH, head_dim), f32),
            pltpu.VMEM((kv_here, width, head_dim), bf16),
            pltpu.VMEM((kv_here, width, 2 * head_dim), bf16),
            pltpu.VMEM((rows_here, 128), f32),
            pltpu.VMEM((ROWS, width), f32),
            pltpu.VMEM((kv_here, head_dim, width), f32),
            pltpu.VMEM((kv_here, head_dim, width), f32),
        ],
        compiler_params=pltpu.CompilerParams(vmem_limit_bytes=40 * 2**20),
    )(
        partner,
        prompt_blocks,
        queries.reshape(-1, head_dim),
        grad_out.reshape(-1, head_dim),
        keys_values.reshape(-1, head_dim),
        segments.reshape(1, rows_here),
        received,
    )
    received_grads = lax.all_to_all(
        slotted(prompt_grad, bin_ids == owner_bin), "seq", split_axis=0, concat_axis=0, tiled=True
    )
    arrived = lax.dynamic_index_in_dim(received_grads, source, 0, keepdims=False)
    if sharing > 1:
        joined = lax.optimization_barrier(jnp.concatenate([own, arrived], axis=0))
        summed = head_total(joined.astype(jnp.float32), sharing)
        own, arrived = summed[:rows_here], summed[rows_here:].astype(jnp.bfloat16)
    head_rows = own[:PMAX].astype(jnp.float32) + arrived.astype(jnp.float32)
    kv_result = lax.dynamic_update_slice(own.astype(jnp.bfloat16), head_rows.astype(jnp.bfloat16), (0, 0))
    return (attention.reshape(queries.shape), query_gradient.reshape(queries.shape), kv_result)


def solution(mesh):
    in_specs = (
        P("seq", "head", None),
        P("seq", None, None, None),
        P("seq", "head", None),
        P("seq"),
        P(),
        P(),
    )
    out_specs = (P("seq", "head", None), P("seq", "head", None), P("seq", "head"))
    return jax.shard_map(body, mesh=mesh, in_specs=in_specs, out_specs=out_specs, check_vma=False)
```

```python
import functools
import math

import jax
import jax.numpy as jnp
from jax import lax
from jax.experimental import pallas as pl
from jax.experimental.pallas import tpu as pltpu
from jax.sharding import PartitionSpec as P

HEADS = 64
KVH = 8
PMAX = 64
BLK = 16
ROWS = 128
PAD = 128
MASKED = -1e30
LOG2E = math.log2(math.e)


def from_partner(value, axis, apart):
    mask = 2**apart
    pairs = [(source, source ^ mask) for source in range(lax.axis_size(axis))]
    return lax.ppermute(value, axis, pairs)


def head_total(block, sharing):
    flat = block.reshape(block.shape[0], -1)
    place = lax.axis_index("head")
    for bit in reversed(range(sharing.bit_length() - 1)):
        half = flat.shape[1] // 2
        mine = place // 2**bit % 2
        kept = lax.dynamic_slice_in_dim(flat, mine * half, half, 1)
        given = lax.dynamic_slice_in_dim(flat, (1 - mine) * half, half, 1)
        got = from_partner(given.astype(jnp.bfloat16), "head", bit).astype(given.dtype)
        flat = kept + got
    return flat


def dot(a, b):
    return jnp.dot(a, b, preferred_element_type=jnp.float32)


def dot_t(a, b):
    return lax.dot_general(a, b, (((1,), (1,)), ((), ())), preferred_element_type=jnp.float32)


def attend(
    heads, kvs, per_kv, chunks, peers, merge, scale,
    partner_ref, blocks_ref, q_ref, do_ref, kv_ref, seg_ref,
    out_ref, dq_ref, own_ref, arrived_ref,
    qf, dof, af, dqf, kvf, kcat, vcat, segc, bias, dkt, dvt,
    parcel, got, grads, got_grads, sent, landed, grads_sent, grads_landed,
):
    group, chunk = pl.program_id(0), pl.program_id(1)
    me = lax.axis_index("seq")
    rows = chunks * ROWS
    width = PAD + rows
    piece = ROWS * heads
    last = chunks - 1

    def prompt_copy(d):
        return pltpu.make_async_remote_copy(
            src_ref=parcel,
            dst_ref=got.at[d],
            send_sem=sent.at[d],
            recv_sem=landed.at[d],
            device_id={"seq": lax.rem(me + d + 1, peers + 1)},
            device_id_type=pl.DeviceIdType.MESH,
        )

    def grad_copy(g, d):
        return pltpu.make_async_remote_copy(
            src_ref=grads.at[g],
            dst_ref=got_grads.at[g, d],
            send_sem=grads_sent.at[g, d],
            recv_sem=grads_landed.at[g, d],
            device_id={"seq": lax.rem(me + d + 1, peers + 1)},
            device_id_type=pl.DeviceIdType.MESH,
        )

    def each_peer(act):
        def one(d, carry):
            act(d)
            return carry
        lax.fori_loop(0, peers, one, 0)

    @pl.when((group == 0) & (chunk == 0))
    def _():
        barrier = pltpu.get_barrier_semaphore()
        each_peer(lambda d: pl.semaphore_signal(
            barrier, inc=1, device_id={"seq": lax.rem(me + d + 1, peers + 1)},
            device_id_type=pl.DeviceIdType.MESH,
        ))
        kv_start = lax.axis_index("head") * heads // (HEADS // KVH)
        early = PMAX * 2 * KVH
        kvf[:early, :] = kv_ref[:early, :].astype(jnp.float32)
        for n in range(2 * kvs):
            at = kv_start + n % kvs + n // kvs * KVH
            parcel[n * PMAX:(n + 1) * PMAX, :] = kvf[pl.ds(at, PMAX, stride=2 * KVH), :].astype(jnp.bfloat16)
        pl.semaphore_wait(barrier, peers)
        each_peer(lambda d: prompt_copy(d).start())
        kvf[early:, :] = kv_ref[early:, :].astype(jnp.float32)
        for g in range(kvs):
            k_rows = kvf[pl.ds(kv_start + g, rows, stride=2 * KVH), :]
            v_rows = kvf[pl.ds(kv_start + g + KVH, rows, stride=2 * KVH), :]
            kcat[g, PAD:, :] = k_rows.astype(jnp.bfloat16)
            vcat[g, PAD:, :128] = v_rows.astype(jnp.bfloat16)
            kcat[g, PMAX:PAD, :] = jnp.zeros((PAD - PMAX, 128), jnp.bfloat16)
            vcat[g, PMAX:PAD, :128] = jnp.zeros((PAD - PMAX, 128), jnp.bfloat16)
            vcat[g, :, 128:] = jnp.ones((width, 128), jnp.bfloat16)
        segc[...] = jnp.broadcast_to(seg_ref[...].astype(jnp.float32), (128, rows)).T
        dkt[...] = jnp.zeros_like(dkt)
        dvt[...] = jnp.zeros_like(dvt)

    @pl.when(group == 0)
    def _():
        here = pl.ds(pl.multiple_of(chunk * piece, piece), piece)
        qf[here, :] = q_ref[...].astype(jnp.float32)
        dof[here, :] = do_ref[...].astype(jnp.float32)

    @pl.when((group == 0) & (chunk == 0))
    def _():
        each_peer(lambda d: prompt_copy(d).wait())
        slot = jnp.maximum(lax.rem(me - partner_ref[me] + peers + 1, peers + 1) - 1, 0)
        for g in range(kvs):
            kcat[g, :PMAX, :] = got[slot, g * PMAX:(g + 1) * PMAX, :]
            vcat[g, :PMAX, :128] = got[slot, (kvs + g) * PMAX:(kvs + g + 1) * PMAX, :]

    def work(c):
        wide = PAD + (c + 1) * ROWS
        live = BLK * blocks_ref[partner_ref[me]]
        column = segc[c * ROWS:(c + 1) * ROWS, :]
        place = lax.broadcasted_iota(jnp.int32, (ROWS, 128), 1)
        row = lax.broadcasted_iota(jnp.int32, (ROWS, 128), 0)
        bias[:, :PAD] = jnp.where((column == 1.0) & (place < live), 0.0, MASKED)
        for j in range(c + 1):
            same = column == seg_ref[:, j * ROWS:(j + 1) * ROWS].astype(jnp.float32)
            if j == c:
                same = same & (place <= row)
            bias[:, PAD + j * ROWS:PAD + (j + 1) * ROWS] = jnp.where(same, 0.0, MASKED)

        def spots(i):
            h = group * per_kv + 2 * i + c * piece
            return pl.ds(h, ROWS, stride=heads), pl.ds(h + 1, ROWS, stride=heads)

        def scores(i):
            first, second = spots(i)
            q32 = jnp.concatenate([qf[first, :], qf[second, :]], axis=0)
            q = q32.astype(jnp.bfloat16)
            return q, dot_t(q, kcat[group, :wide, :])

        def softmax(i, q, s):
            first, second = spots(i)
            b = bias[:, :wide]
            t = s * (scale * LOG2E) + jnp.concatenate([b, b], axis=0)
            p = jnp.exp2(t - jnp.max(t, axis=1, keepdims=True))
            pb = p.astype(jnp.bfloat16)
            mixed = dot(pb, vcat[group, :wide, :])
            inverse = 1.0 / mixed[:, 128:]
            attention = (mixed[:, :128] * inverse).astype(jnp.bfloat16).astype(jnp.float32)
            af[first, :] = attention[:ROWS]
            af[second, :] = attention[ROWS:]
            do = jnp.concatenate([dof[first, :], dof[second, :]], axis=0)
            dos = (do * inverse).astype(jnp.bfloat16)
            delta = jnp.sum(dos.astype(jnp.float32) * attention, axis=1, keepdims=True)
            dp = dot_t(dos, vcat[group, :wide, :128])
            ds = (p * (dp - delta)).astype(jnp.bfloat16)
            return q, pb, dos, ds

        def gradients(i, q, pb, dos, ds):
            first, second = spots(i)
            dq = dot(ds, kcat[group, :wide, :]) * scale
            dqf[first, :] = dq[:ROWS]
            dqf[second, :] = dq[ROWS:]
            dkt[group, :, :wide] += dot(q.T, ds)
            dvt[group, :, :wide] += dot(dos.T, pb)

        pairs = per_kv // 2
        scored, soft = {}, {}
        for i in range(pairs + 2):
            if i < pairs:
                scored[i] = scores(i)
            if 0 <= i - 1 < pairs:
                soft[i - 1] = softmax(i - 1, *scored.pop(i - 1))
            if 0 <= i - 2 < pairs:
                gradients(i - 2, *soft.pop(i - 2))

    for c in range(chunks):
        pl.when(chunk == c)(functools.partial(work, c))

    @pl.when(group == kvs - 1)
    def _():
        here = pl.ds(pl.multiple_of(chunk * piece, piece), piece)
        out_ref[...] = af[here, :].astype(jnp.bfloat16)
        dq_ref[...] = dqf[here, :].astype(jnp.bfloat16)

    for g in range(kvs):
        @pl.when((group == g) & (chunk == last))
        def _():
            for part, total in ((0, dkt), (1, dvt)):
                grads[g, :, part * 128:(part + 1) * 128] = (
                    (total[g, :, :PAD] * (1.0 if part else scale)).T[:PMAX].astype(jnp.bfloat16)
                )
            each_peer(lambda d: grad_copy(g, d).start())
            for part, total in ((0, dkt), (1, dvt)):
                at = (2 * g + part) * 128
                own_ref[:, at:at + 128] = (
                    (total[g, :, PAD:] * (1.0 if part else scale)).T.astype(jnp.bfloat16)
                )

    @pl.when((group == kvs - 1) & (chunk == last))
    def _():
        slot = jnp.int32(0)
        for b in range(peers + 1):
            slot = jnp.where(partner_ref[b] == me, lax.rem(me - b + peers + 1, peers + 1) - 1, slot)
        slot = jnp.maximum(slot, 0)
        for g in range(kvs):
            each_peer(lambda d: grad_copy(g, d).wait())
        for g in range(kvs):
            block = got_grads[g, slot]
            at = slice(g * 256, (g + 1) * 256)
            arrived_ref[:, at] = block
            if merge:
                own_ref[:PMAX, at] = (
                    own_ref[:PMAX, at].astype(jnp.float32) + block.astype(jnp.float32)
                ).astype(jnp.bfloat16)


def body(queries, keys_values, grad_out, segments, partner, prompt_blocks):
    rows_here, heads_here, head_dim = queries.shape
    group_size = HEADS // KVH
    kv_here = max(1, heads_here // group_size)
    per_kv = heads_here // kv_here
    sharing = max(1, group_size // heads_here)
    peers = lax.axis_size("seq") - 1
    chunks = rows_here // ROWS
    width = PAD + rows_here
    last = chunks - 1
    block_in = pl.BlockSpec((ROWS * heads_here, head_dim), lambda g, c: (jnp.where(g == 0, c, last), 0))
    block_out = pl.BlockSpec((ROWS * heads_here, head_dim), lambda g, c: (jnp.where(g == kv_here - 1, c, 0), 0))
    whole = pl.BlockSpec(memory_space=pltpu.VMEM)
    flat = jax.ShapeDtypeStruct((rows_here * heads_here, head_dim), jnp.bfloat16)
    f32, bf16 = jnp.float32, jnp.bfloat16
    attention, query_gradient, own, arrived = pl.pallas_call(
        functools.partial(
            attend, heads_here, kv_here, per_kv, chunks, peers, sharing == 1, 1.0 / math.sqrt(head_dim)
        ),
        grid=(kv_here, chunks),
        in_specs=[pl.BlockSpec(memory_space=pltpu.SMEM)] * 2 + [block_in, block_in, whole, whole],
        out_specs=[block_out, block_out, whole, whole],
        out_shape=[
            flat,
            flat,
            jax.ShapeDtypeStruct((rows_here, kv_here * 2 * head_dim), bf16),
            jax.ShapeDtypeStruct((PMAX, kv_here * 2 * head_dim), bf16),
        ],
        scratch_shapes=[pltpu.VMEM((rows_here * heads_here, head_dim), f32)] * 4
        + [
            pltpu.VMEM((rows_here * 2 * KVH, head_dim), f32),
            pltpu.VMEM((kv_here, width, head_dim), bf16),
            pltpu.VMEM((kv_here, width, 2 * head_dim), bf16),
            pltpu.VMEM((rows_here, 128), f32),
            pltpu.VMEM((ROWS, width), f32),
            pltpu.VMEM((kv_here, head_dim, width), f32),
            pltpu.VMEM((kv_here, head_dim, width), f32),
            pltpu.VMEM((2 * kv_here * PMAX, head_dim), bf16),
            pltpu.VMEM((peers, 2 * kv_here * PMAX, head_dim), bf16),
            pltpu.VMEM((kv_here, PMAX, 2 * head_dim), bf16),
            pltpu.VMEM((kv_here, peers, PMAX, 2 * head_dim), bf16),
            pltpu.SemaphoreType.DMA((peers,)),
            pltpu.SemaphoreType.DMA((peers,)),
            pltpu.SemaphoreType.DMA((kv_here, peers)),
            pltpu.SemaphoreType.DMA((kv_here, peers)),
        ],
        compiler_params=pltpu.CompilerParams(
            vmem_limit_bytes=56 * 2**20, collective_id=0, has_side_effects=True
        ),
    )(
        partner,
        prompt_blocks,
        queries.reshape(-1, head_dim),
        grad_out.reshape(-1, head_dim),
        keys_values.reshape(-1, head_dim),
        segments.reshape(1, rows_here),
    )
    if sharing > 1:
        joined = lax.optimization_barrier(jnp.concatenate([own, arrived], axis=0))
        summed = head_total(joined.astype(jnp.float32), sharing)
        own, arrived = summed[:rows_here], summed[rows_here:].astype(jnp.bfloat16)
        head_rows = own[:PMAX] + arrived.astype(jnp.float32)
        own = jnp.concatenate([head_rows, own[PMAX:]], axis=0).astype(jnp.bfloat16)
    return (attention.reshape(queries.shape), query_gradient.reshape(queries.shape), own)


def solution(mesh):
    in_specs = (
        P("seq", "head", None),
        P("seq", None, None, None),
        P("seq", "head", None),
        P("seq"),
        P(),
        P(),
    )
    out_specs = (P("seq", "head", None), P("seq", "head", None), P("seq", "head"))
    return jax.shard_map(body, mesh=mesh, in_specs=in_specs, out_specs=out_specs, check_vma=False)
```

```python
import functools
import math

import jax
import jax.numpy as jnp
from jax import lax
from jax.experimental import pallas as pl
from jax.experimental.pallas import tpu as pltpu
from jax.sharding import PartitionSpec as P

HEADS = 64
KVH = 8
PMAX = 64
BLK = 16
ROWS = 128
PAD = 128
MASKED = -1e30
LOG2E = math.log2(math.e)


def from_partner(value, axis, apart):
    mask = 2**apart
    pairs = [(source, source ^ mask) for source in range(lax.axis_size(axis))]
    return lax.ppermute(value, axis, pairs)


def head_total(block, sharing):
    flat = block.reshape(block.shape[0], -1)
    place = lax.axis_index("head")
    for bit in reversed(range(sharing.bit_length() - 1)):
        half = flat.shape[1] // 2
        mine = place // 2**bit % 2
        kept = lax.dynamic_slice_in_dim(flat, mine * half, half, 1)
        given = lax.dynamic_slice_in_dim(flat, (1 - mine) * half, half, 1)
        got = from_partner(given.astype(jnp.bfloat16), "head", bit).astype(given.dtype)
        flat = kept + got
    return flat


def dot(a, b):
    return jnp.dot(a, b, preferred_element_type=jnp.float32)


def dot_t(a, b):
    return lax.dot_general(a, b, (((1,), (1,)), ((), ())), preferred_element_type=jnp.float32)


def attend(
    heads, kvs, per_kv, chunks, peers, merge, scale,
    partner_ref, blocks_ref, q_hbm, do_hbm, kv_hbm, seg_ref,
    out_ref, dq_ref, own_ref, arrived_ref,
    q_ref, do_ref, kv_ref,
    qf, dof, dqf, af, kcat, vcat, segc, bias, dkt, dvt,
    early_s, early_dp, kept_pb, kept_ds, kept_dos,
    parcel, got, grads, got_grads, sent, landed, grads_sent, grads_landed, kv_sem, q_sem, do_sem,
):
    me = lax.axis_index("seq")
    kvf = af
    rows = chunks * ROWS
    width = PAD + rows
    piece = ROWS * heads
    last = chunks - 1

    def prompt_copy(d):
        return pltpu.make_async_remote_copy(
            src_ref=parcel,
            dst_ref=got.at[d],
            send_sem=sent.at[d],
            recv_sem=landed.at[d],
            device_id={"seq": lax.rem(me + d + 1, peers + 1)},
            device_id_type=pl.DeviceIdType.MESH,
        )

    def grad_copy(g, d):
        return pltpu.make_async_remote_copy(
            src_ref=grads.at[g],
            dst_ref=got_grads.at[g, d],
            send_sem=grads_sent.at[g, d],
            recv_sem=grads_landed.at[g, d],
            device_id={"seq": lax.rem(me + d + 1, peers + 1)},
            device_id_type=pl.DeviceIdType.MESH,
        )

    def each_peer(act):
        def one(d, carry):
            act(d)
            return carry
        lax.fori_loop(0, peers, one, 0)

    def separately(act):
        pl.when(me >= 0)(act)

    def span(c):
        return pl.ds(c * piece, piece)

    early = PMAX * 2 * KVH
    loads = [
        pltpu.make_async_copy(kv_hbm.at[pl.ds(0, early)], kv_ref.at[pl.ds(0, early)], kv_sem.at[0]),
        pltpu.make_async_copy(
            kv_hbm.at[pl.ds(early, rows * 2 * KVH - early)],
            kv_ref.at[pl.ds(early, rows * 2 * KVH - early)],
            kv_sem.at[1],
        ),
    ]
    q_loads = [pltpu.make_async_copy(q_hbm.at[span(c)], q_ref.at[span(c)], q_sem.at[c]) for c in range(chunks)]
    do_loads = [pltpu.make_async_copy(do_hbm.at[span(c)], do_ref.at[span(c)], do_sem.at[c]) for c in range(chunks)]
    for load in loads + q_loads + do_loads:
        load.start()
    barrier = pltpu.get_barrier_semaphore()
    each_peer(lambda d: pl.semaphore_signal(
        barrier, inc=1, device_id={"seq": lax.rem(me + d + 1, peers + 1)},
        device_id_type=pl.DeviceIdType.MESH,
    ))
    kv_start = lax.axis_index("head") * heads // (HEADS // KVH)
    loads[0].wait()
    kvf[:early, :] = kv_ref[:early, :].astype(jnp.float32)
    for n in range(2 * kvs):
        at = kv_start + n % kvs + n // kvs * KVH
        parcel[n * PMAX:(n + 1) * PMAX, :] = kvf[pl.ds(at, PMAX, stride=2 * KVH), :].astype(jnp.bfloat16)
    pl.semaphore_wait(barrier, peers)
    each_peer(lambda d: prompt_copy(d).start())
    loads[1].wait()
    kvf[early:, :] = kv_ref[early:, :].astype(jnp.float32)
    for g in range(kvs):
        k_rows = kvf[pl.ds(kv_start + g, rows, stride=2 * KVH), :]
        v_rows = kvf[pl.ds(kv_start + g + KVH, rows, stride=2 * KVH), :]
        kcat[g, PAD:, :] = k_rows.astype(jnp.bfloat16)
        vcat[g, PAD:, :128] = v_rows.astype(jnp.bfloat16)
        kcat[g, PMAX:PAD, :] = jnp.zeros((PAD - PMAX, 128), jnp.bfloat16)
        vcat[g, PMAX:PAD, :128] = jnp.zeros((PAD - PMAX, 128), jnp.bfloat16)
        vcat[g, :, 128:] = jnp.ones((width, 128), jnp.bfloat16)
    segc[...] = jnp.broadcast_to(seg_ref[...].astype(jnp.float32), (128, rows)).T
    dkt[...] = jnp.zeros_like(dkt)
    dvt[...] = jnp.zeros_like(dvt)

    pairs = per_kv // 2

    def spots(g, c, i):
        h = g * per_kv + 2 * i + c * piece
        return pl.ds(h, ROWS, stride=heads), pl.ds(h + 1, ROWS, stride=heads)

    def both(ref, g, c, i):
        first, second = spots(g, c, i)
        return jnp.concatenate([ref[first, :], ref[second, :]], axis=0)

    def prepare(c):
        q_loads[c].wait()
        do_loads[c].wait()
        qf[span(c), :] = q_ref[span(c), :].astype(jnp.float32)
        dof[span(c), :] = do_ref[span(c), :].astype(jnp.float32)
        size = (c + 1) * ROWS
        start = c * (c + 1) // 2 * ROWS
        for i in range(pairs):
            q = both(qf, 0, c, i).astype(jnp.bfloat16)
            do = both(dof, 0, c, i).astype(jnp.bfloat16)
            early_s[i, :, start:start + size] = dot_t(q, kcat[0, PAD:PAD + size, :])
            early_dp[i, :, start:start + size] = dot_t(do, vcat[0, PAD:PAD + size, :128])

    for c in range(chunks):
        separately(functools.partial(prepare, c))

    each_peer(lambda d: prompt_copy(d).wait())
    slot = jnp.maximum(lax.rem(me - partner_ref[me] + peers + 1, peers + 1) - 1, 0)
    for g in range(kvs):
        kcat[g, :PMAX, :] = got[slot, g * PMAX:(g + 1) * PMAX, :]
        vcat[g, :PMAX, :128] = got[slot, (kvs + g) * PMAX:(kvs + g + 1) * PMAX, :]

    def work(g, c):
        wide = PAD + (c + 1) * ROWS
        size = (c + 1) * ROWS
        start = c * (c + 1) // 2 * ROWS
        final = g == kvs - 1 and c == last
        live = BLK * blocks_ref[partner_ref[me]]
        column = segc[c * ROWS:(c + 1) * ROWS, :]
        place = lax.broadcasted_iota(jnp.int32, (ROWS, 128), 1)
        row = lax.broadcasted_iota(jnp.int32, (ROWS, 128), 0)
        bias[:, :PAD] = jnp.where((column == 1.0) & (place < live), 0.0, MASKED)
        for j in range(c + 1):
            same = column == seg_ref[:, j * ROWS:(j + 1) * ROWS].astype(jnp.float32)
            if j == c:
                same = same & (place <= row)
            bias[:, PAD + j * ROWS:PAD + (j + 1) * ROWS] = jnp.where(same, 0.0, MASKED)

        def scores(i):
            q = both(qf, g, c, i).astype(jnp.bfloat16)
            do = both(dof, g, c, i)
            low = do.astype(jnp.bfloat16)
            if g == 0:
                s = jnp.concatenate([dot_t(q, kcat[g, :PAD, :]), early_s[i, :, start:start + size]], axis=1)
                dp = jnp.concatenate([dot_t(low, vcat[g, :PAD, :128]), early_dp[i, :, start:start + size]], axis=1)
            else:
                s = dot_t(q, kcat[g, :wide, :])
                dp = dot_t(low, vcat[g, :wide, :128])
            return q, do, s, dp

        def softmax(i, q, do, s, dp):
            first, second = spots(g, c, i)
            b = bias[:, :wide]
            t = s * (scale * LOG2E) + jnp.concatenate([b, b], axis=0)
            p = jnp.exp2(t - jnp.max(t, axis=1, keepdims=True))
            pb = p.astype(jnp.bfloat16)
            mixed = dot(pb, vcat[g, :wide, :])
            inverse = 1.0 / mixed[:, 128:]
            attention = (mixed[:, :128] * inverse).astype(jnp.bfloat16).astype(jnp.float32)
            af[first, :] = attention[:ROWS]
            af[second, :] = attention[ROWS:]
            dos = (do * inverse).astype(jnp.bfloat16)
            delta = jnp.sum(do * attention, axis=1, keepdims=True)
            ds = (p * inverse[:, :1] * (dp - delta)).astype(jnp.bfloat16)
            return q, pb, dos, ds

        def query_part(i, ds):
            first, second = spots(g, c, i)
            dq = dot(ds, kcat[g, :wide, :]) * scale
            dqf[first, :] = dq[:ROWS]
            dqf[second, :] = dq[ROWS:]

        def gradients(i, q, pb, dos, ds):
            if final:
                kept_pb[i], kept_ds[i], kept_dos[i] = pb, ds, dos
                dkt[g, :, :PAD] += dot(q.T, ds[:, :PAD])
                dvt[g, :, :PAD] += dot(dos.T, pb[:, :PAD])
            else:
                query_part(i, ds)
                dkt[g, :, :wide] += dot(q.T, ds)
                dvt[g, :, :wide] += dot(dos.T, pb)

        scored, soft = {}, {}
        for i in range(pairs + 2):
            if i < pairs:
                scored[i] = scores(i)
            if 0 <= i - 1 < pairs:
                soft[i - 1] = softmax(i - 1, *scored.pop(i - 1))
            if 0 <= i - 2 < pairs:
                gradients(i - 2, *soft.pop(i - 2))
        if c == last:
            for part, total in ((0, dkt), (1, dvt)):
                grads[g, :, part * 128:(part + 1) * 128] = (
                    (total[g, :, :PAD] * (1.0 if part else scale)).T[:PMAX].astype(jnp.bfloat16)
                )
            each_peer(lambda d: grad_copy(g, d).start())
        if final:
            for i in range(pairs):
                q = both(qf, g, c, i).astype(jnp.bfloat16)
                ds, pb, dos = kept_ds[i], kept_pb[i], kept_dos[i]
                query_part(i, ds)
                dkt[g, :, PAD:] += dot(q.T, ds[:, PAD:])
                dvt[g, :, PAD:] += dot(dos.T, pb[:, PAD:])
        if c == last:
            for part, total in ((0, dkt), (1, dvt)):
                at = (2 * g + part) * 128
                own_ref[:, at:at + 128] = (
                    (total[g, :, PAD:] * (1.0 if part else scale)).T.astype(jnp.bfloat16)
                )
        if g == kvs - 1:
            out_ref[span(c), :] = af[span(c), :].astype(jnp.bfloat16)
            dq_ref[span(c), :] = dqf[span(c), :].astype(jnp.bfloat16)

    for g in range(kvs):
        for c in range(chunks):
            separately(functools.partial(work, g, c))

    slot = jnp.int32(0)
    for b in range(peers + 1):
        slot = jnp.where(partner_ref[b] == me, lax.rem(me - b + peers + 1, peers + 1) - 1, slot)
    slot = jnp.maximum(slot, 0)
    for g in range(kvs):
        each_peer(lambda d: grad_copy(g, d).wait())
    for g in range(kvs):
        block = got_grads[g, slot]
        at = slice(g * 256, (g + 1) * 256)
        arrived_ref[:, at] = block
        if merge:
            own_ref[:PMAX, at] = (
                own_ref[:PMAX, at].astype(jnp.float32) + block.astype(jnp.float32)
            ).astype(jnp.bfloat16)


def body(queries, keys_values, grad_out, segments, partner, prompt_blocks):
    rows_here, heads_here, head_dim = queries.shape
    group_size = HEADS // KVH
    kv_here = max(1, heads_here // group_size)
    per_kv = heads_here // kv_here
    sharing = max(1, group_size // heads_here)
    peers = lax.axis_size("seq") - 1
    chunks = rows_here // ROWS
    width = PAD + rows_here
    pairs = per_kv // 2
    far = pl.BlockSpec(memory_space=pl.ANY)
    whole = pl.BlockSpec(memory_space=pltpu.VMEM)
    flat = jax.ShapeDtypeStruct((rows_here * heads_here, head_dim), jnp.bfloat16)
    f32, bf16 = jnp.float32, jnp.bfloat16
    attention, query_gradient, own, arrived = pl.pallas_call(
        functools.partial(
            attend, heads_here, kv_here, per_kv, chunks, peers, sharing == 1, 1.0 / math.sqrt(head_dim)
        ),
        in_specs=[pl.BlockSpec(memory_space=pltpu.SMEM)] * 2 + [far, far, far, whole],
        out_specs=[whole] * 4,
        out_shape=[
            flat,
            flat,
            jax.ShapeDtypeStruct((rows_here, kv_here * 2 * head_dim), bf16),
            jax.ShapeDtypeStruct((PMAX, kv_here * 2 * head_dim), bf16),
        ],
        scratch_shapes=[pltpu.VMEM((rows_here * heads_here, head_dim), bf16)] * 2
        + [pltpu.VMEM((rows_here * 2 * KVH, head_dim), bf16)]
        + [pltpu.VMEM((rows_here * heads_here, head_dim), f32)] * 3
        + [
            pltpu.VMEM((rows_here * max(heads_here, 2 * KVH), head_dim), f32),
            pltpu.VMEM((kv_here, width, head_dim), bf16),
            pltpu.VMEM((kv_here, width, 2 * head_dim), bf16),
            pltpu.VMEM((rows_here, 128), f32),
            pltpu.VMEM((ROWS, width), f32),
            pltpu.VMEM((kv_here, head_dim, width), f32),
            pltpu.VMEM((kv_here, head_dim, width), f32),
            pltpu.VMEM((pairs, 2 * ROWS, chunks * (chunks + 1) // 2 * ROWS), f32),
            pltpu.VMEM((pairs, 2 * ROWS, chunks * (chunks + 1) // 2 * ROWS), f32),
            pltpu.VMEM((pairs, 2 * ROWS, width), bf16),
            pltpu.VMEM((pairs, 2 * ROWS, width), bf16),
            pltpu.VMEM((pairs, 2 * ROWS, head_dim), bf16),
            pltpu.VMEM((2 * kv_here * PMAX, head_dim), bf16),
            pltpu.VMEM((peers, 2 * kv_here * PMAX, head_dim), bf16),
            pltpu.VMEM((kv_here, PMAX, 2 * head_dim), bf16),
            pltpu.VMEM((kv_here, peers, PMAX, 2 * head_dim), bf16),
            pltpu.SemaphoreType.DMA((peers,)),
            pltpu.SemaphoreType.DMA((peers,)),
            pltpu.SemaphoreType.DMA((kv_here, peers)),
            pltpu.SemaphoreType.DMA((kv_here, peers)),
            pltpu.SemaphoreType.DMA((2,)),
            pltpu.SemaphoreType.DMA((chunks,)),
            pltpu.SemaphoreType.DMA((chunks,)),
        ],
        compiler_params=pltpu.CompilerParams(
            vmem_limit_bytes=48 * 2**20, collective_id=0, has_side_effects=True
        ),
    )(
        partner,
        prompt_blocks,
        queries.reshape(-1, head_dim),
        grad_out.reshape(-1, head_dim),
        keys_values.reshape(-1, head_dim),
        segments.reshape(1, rows_here),
    )
    if sharing > 1:
        joined = lax.optimization_barrier(jnp.concatenate([own, arrived], axis=0))
        summed = head_total(joined.astype(jnp.float32), sharing)
        own, arrived = summed[:rows_here], summed[rows_here:].astype(jnp.bfloat16)
        head_rows = own[:PMAX] + arrived.astype(jnp.float32)
        own = jnp.concatenate([head_rows, own[PMAX:]], axis=0).astype(jnp.bfloat16)
    return (attention.reshape(queries.shape), query_gradient.reshape(queries.shape), own)


def solution(mesh):
    in_specs = (
        P("seq", "head", None),
        P("seq", None, None, None),
        P("seq", "head", None),
        P("seq"),
        P(),
        P(),
    )
    out_specs = (P("seq", "head", None), P("seq", "head", None), P("seq", "head"))
    return jax.shard_map(body, mesh=mesh, in_specs=in_specs, out_specs=out_specs, check_vma=False)
```

```python
import functools
import math

import jax
import jax.numpy as jnp
from jax import lax
from jax.experimental import pallas as pl
from jax.experimental.pallas import tpu as pltpu
from jax.sharding import PartitionSpec as P

HEADS = 64
KVH = 8
PMAX = 64
BLK = 16
ROWS = 128
PAD = 128
TILE = 32
MASKED = -1e30
LOG2E = math.log2(math.e)


def from_partner(value, axis, apart):
    mask = 2**apart
    pairs = [(source, source ^ mask) for source in range(lax.axis_size(axis))]
    return lax.ppermute(value, axis, pairs)


def head_total(block, sharing):
    flat = block.reshape(block.shape[0], -1)
    place = lax.axis_index("head")
    for bit in reversed(range(sharing.bit_length() - 1)):
        half = flat.shape[1] // 2
        mine = place // 2**bit % 2
        kept = lax.dynamic_slice_in_dim(flat, mine * half, half, 1)
        given = lax.dynamic_slice_in_dim(flat, (1 - mine) * half, half, 1)
        got = from_partner(given.astype(jnp.bfloat16), "head", bit).astype(given.dtype)
        flat = kept + got
    return flat


def dot(a, b):
    return jnp.dot(a, b, preferred_element_type=jnp.float32)


def dot_t(a, b):
    return lax.dot_general(a, b, (((1,), (1,)), ((), ())), preferred_element_type=jnp.float32)


def attend(
    heads, kvs, per_kv, chunks, peers, merge, scale,
    partner_ref, blocks_ref, q_hbm, do_hbm, kv_hbm, seg_ref,
    out_ref, dq_ref, own_ref, arrived_ref,
    q_ref, do_ref, kv_ref,
    qf, dof, dqf, af, kcat, vcat, segc, bias, dkt, dvt,
    early_s, early_dp, kept_pb, kept_ds, kept_dos,
    parcel, got, grads, got_grads, sent, landed, grads_sent, grads_landed, kv_sem, q_sem, do_sem,
):
    me = lax.axis_index("seq")
    kvf = af
    rows = chunks * ROWS
    width = PAD + rows
    piece = ROWS * heads
    last = chunks - 1

    def prompt_copy(d):
        return pltpu.make_async_remote_copy(
            src_ref=parcel,
            dst_ref=got.at[d],
            send_sem=sent.at[d],
            recv_sem=landed.at[d],
            device_id={"seq": lax.rem(me + d + 1, peers + 1)},
            device_id_type=pl.DeviceIdType.MESH,
        )

    def grad_copy(g, d):
        return pltpu.make_async_remote_copy(
            src_ref=grads.at[g],
            dst_ref=got_grads.at[g, d],
            send_sem=grads_sent.at[g, d],
            recv_sem=grads_landed.at[g, d],
            device_id={"seq": lax.rem(me + d + 1, peers + 1)},
            device_id_type=pl.DeviceIdType.MESH,
        )

    def each_peer(act):
        def one(d, carry):
            act(d)
            return carry
        lax.fori_loop(0, peers, one, 0)

    def separately(act):
        pl.when(me >= 0)(act)

    def span(c):
        return pl.ds(c * piece, piece)

    early = PMAX * 2 * KVH
    loads = [
        pltpu.make_async_copy(kv_hbm.at[pl.ds(0, early)], kv_ref.at[pl.ds(0, early)], kv_sem.at[0]),
        pltpu.make_async_copy(
            kv_hbm.at[pl.ds(early, rows * 2 * KVH - early)],
            kv_ref.at[pl.ds(early, rows * 2 * KVH - early)],
            kv_sem.at[1],
        ),
    ]
    q_loads = [pltpu.make_async_copy(q_hbm.at[span(c)], q_ref.at[span(c)], q_sem.at[c]) for c in range(chunks)]
    do_loads = [pltpu.make_async_copy(do_hbm.at[span(c)], do_ref.at[span(c)], do_sem.at[c]) for c in range(chunks)]
    for load in loads + q_loads + do_loads:
        load.start()
    barrier = pltpu.get_barrier_semaphore()
    each_peer(lambda d: pl.semaphore_signal(
        barrier, inc=1, device_id={"seq": lax.rem(me + d + 1, peers + 1)},
        device_id_type=pl.DeviceIdType.MESH,
    ))
    kv_start = lax.axis_index("head") * heads // (HEADS // KVH)
    loads[0].wait()
    kvf[:early, :] = kv_ref[:early, :].astype(jnp.float32)
    for n in range(2 * kvs):
        at = kv_start + n % kvs + n // kvs * KVH
        parcel[n * PMAX:(n + 1) * PMAX, :] = kvf[pl.ds(at, PMAX, stride=2 * KVH), :].astype(jnp.bfloat16)
    pl.semaphore_wait(barrier, peers)
    each_peer(lambda d: prompt_copy(d).start())
    loads[1].wait()
    kvf[early:, :] = kv_ref[early:, :].astype(jnp.float32)
    for g in range(kvs):
        k_rows = kvf[pl.ds(kv_start + g, rows, stride=2 * KVH), :]
        v_rows = kvf[pl.ds(kv_start + g + KVH, rows, stride=2 * KVH), :]
        kcat[g, PAD:, :] = k_rows.astype(jnp.bfloat16)
        vcat[g, PAD:, :128] = v_rows.astype(jnp.bfloat16)
        kcat[g, PMAX:PAD, :] = jnp.zeros((PAD - PMAX, 128), jnp.bfloat16)
        vcat[g, PMAX:PAD, :128] = jnp.zeros((PAD - PMAX, 128), jnp.bfloat16)
        vcat[g, :, 128:] = jnp.ones((width, 128), jnp.bfloat16)
    segc[...] = jnp.broadcast_to(seg_ref[...].astype(jnp.float32), (128, rows)).T
    dkt[...] = jnp.zeros_like(dkt)
    dvt[...] = jnp.zeros_like(dvt)

    pairs = per_kv // 2

    def spots(g, c, i):
        h = g * per_kv + 2 * i + c * piece
        return pl.ds(h, ROWS, stride=heads), pl.ds(h + 1, ROWS, stride=heads)

    def both(ref, g, c, i):
        first, second = spots(g, c, i)
        return jnp.concatenate([ref[first, :], ref[second, :]], axis=0)

    def prepare(c):
        q_loads[c].wait()
        do_loads[c].wait()
        qf[span(c), :] = q_ref[span(c), :].astype(jnp.float32)
        dof[span(c), :] = do_ref[span(c), :].astype(jnp.float32)
        size = (c + 1) * ROWS
        start = c * (c + 1) // 2 * ROWS
        for i in range(pairs):
            q = both(qf, 0, c, i).astype(jnp.bfloat16)
            do = both(dof, 0, c, i).astype(jnp.bfloat16)
            early_s[i, :, start:start + size] = dot_t(q, kcat[0, PAD:PAD + size, :])
            early_dp[i, :, start:start + size] = dot_t(do, vcat[0, PAD:PAD + size, :128])

    for c in range(chunks):
        separately(functools.partial(prepare, c))

    each_peer(lambda d: prompt_copy(d).wait())
    slot = jnp.maximum(lax.rem(me - partner_ref[me] + peers + 1, peers + 1) - 1, 0)
    for g in range(kvs):
        kcat[g, :PMAX, :] = got[slot, g * PMAX:(g + 1) * PMAX, :]
        vcat[g, :PMAX, :128] = got[slot, (kvs + g) * PMAX:(kvs + g + 1) * PMAX, :]

    def work(g, c):
        wide = PAD + (c + 1) * ROWS
        size = (c + 1) * ROWS
        start = c * (c + 1) // 2 * ROWS
        final = g == kvs - 1 and c == last
        live = BLK * blocks_ref[partner_ref[me]]
        column = segc[c * ROWS:(c + 1) * ROWS, :]
        place = lax.broadcasted_iota(jnp.int32, (ROWS, 128), 1)
        row = lax.broadcasted_iota(jnp.int32, (ROWS, 128), 0)
        bias[:, :PAD] = jnp.where((column == 1.0) & (place < live), 0.0, MASKED)
        for j in range(c + 1):
            same = column == seg_ref[:, j * ROWS:(j + 1) * ROWS].astype(jnp.float32)
            if j == c:
                same = same & (place <= row)
            bias[:, PAD + j * ROWS:PAD + (j + 1) * ROWS] = jnp.where(same, 0.0, MASKED)

        def scores(i):
            q = both(qf, g, c, i).astype(jnp.bfloat16)
            do = both(dof, g, c, i)
            low = do.astype(jnp.bfloat16)
            if g == 0:
                s = jnp.concatenate([dot_t(q, kcat[g, :PAD, :]), early_s[i, :, start:start + size]], axis=1)
                dp = jnp.concatenate([dot_t(low, vcat[g, :PAD, :128]), early_dp[i, :, start:start + size]], axis=1)
            else:
                s = dot_t(q, kcat[g, :wide, :])
                dp = dot_t(low, vcat[g, :wide, :128])
            return q, do, s, dp

        def softmax(i, q, do, s, dp):
            first, second = spots(g, c, i)
            tiles = [slice(r, r + TILE) for r in range(0, 2 * ROWS, TILE)]
            low = []
            for tile in tiles:
                row = tile.start % ROWS
                t = s[tile] * (scale * LOG2E) + bias[row:row + TILE, :wide]
                low.append(jnp.exp2(t - jnp.max(t, axis=1, keepdims=True)).astype(jnp.bfloat16))
            pb = jnp.concatenate(low, axis=0)
            mixed = dot(pb, vcat[g, :wide, :])
            outs, doss, dss = [], [], []
            for tile, p in zip(tiles, low):
                inverse = 1.0 / mixed[tile, 128:]
                attention = (mixed[tile, :128] * inverse).astype(jnp.bfloat16).astype(jnp.float32)
                outs.append(attention)
                doss.append((do[tile] * inverse).astype(jnp.bfloat16))
                delta = jnp.sum(do[tile] * attention, axis=1, keepdims=True)
                dss.append(p * ((dp[tile] - delta) * inverse[:, :1]).astype(jnp.bfloat16))
            attention = jnp.concatenate(outs, axis=0)
            af[first, :] = attention[:ROWS]
            af[second, :] = attention[ROWS:]
            return q, pb, jnp.concatenate(doss, axis=0), jnp.concatenate(dss, axis=0)

        def query_part(i, ds):
            first, second = spots(g, c, i)
            dq = dot(ds, kcat[g, :wide, :]) * scale
            dqf[first, :] = dq[:ROWS]
            dqf[second, :] = dq[ROWS:]

        def gradients(i, q, pb, dos, ds):
            if final:
                kept_pb[i], kept_ds[i], kept_dos[i] = pb, ds, dos
                dkt[g, :, :PAD] += dot(q.T, ds[:, :PAD])
                dvt[g, :, :PAD] += dot(dos.T, pb[:, :PAD])
            else:
                query_part(i, ds)
                dkt[g, :, :wide] += dot(q.T, ds)
                dvt[g, :, :wide] += dot(dos.T, pb)

        scored, soft = {}, {}
        for i in range(pairs + 2):
            if i < pairs:
                scored[i] = scores(i)
            if 0 <= i - 1 < pairs:
                soft[i - 1] = softmax(i - 1, *scored.pop(i - 1))
            if 0 <= i - 2 < pairs:
                gradients(i - 2, *soft.pop(i - 2))
        if c == last:
            for part, total in ((0, dkt), (1, dvt)):
                grads[g, :, part * 128:(part + 1) * 128] = (
                    (total[g, :, :PAD] * (1.0 if part else scale)).T[:PMAX].astype(jnp.bfloat16)
                )
            each_peer(lambda d: grad_copy(g, d).start())
        if final:
            for i in range(pairs):
                q = both(qf, g, c, i).astype(jnp.bfloat16)
                ds, pb, dos = kept_ds[i], kept_pb[i], kept_dos[i]
                query_part(i, ds)
                dkt[g, :, PAD:] += dot(q.T, ds[:, PAD:])
                dvt[g, :, PAD:] += dot(dos.T, pb[:, PAD:])
        if c == last:
            for part, total in ((0, dkt), (1, dvt)):
                at = (2 * g + part) * 128
                own_ref[:, at:at + 128] = (
                    (total[g, :, PAD:] * (1.0 if part else scale)).T.astype(jnp.bfloat16)
                )
        if g == kvs - 1:
            out_ref[span(c), :] = af[span(c), :].astype(jnp.bfloat16)
            dq_ref[span(c), :] = dqf[span(c), :].astype(jnp.bfloat16)

    for g in range(kvs):
        for c in range(chunks):
            separately(functools.partial(work, g, c))

    slot = jnp.int32(0)
    for b in range(peers + 1):
        slot = jnp.where(partner_ref[b] == me, lax.rem(me - b + peers + 1, peers + 1) - 1, slot)
    slot = jnp.maximum(slot, 0)
    for g in range(kvs):
        each_peer(lambda d: grad_copy(g, d).wait())
    for g in range(kvs):
        block = got_grads[g, slot]
        at = slice(g * 256, (g + 1) * 256)
        arrived_ref[:, at] = block
        if merge:
            own_ref[:PMAX, at] = (
                own_ref[:PMAX, at].astype(jnp.float32) + block.astype(jnp.float32)
            ).astype(jnp.bfloat16)


def body(queries, keys_values, grad_out, segments, partner, prompt_blocks):
    rows_here, heads_here, head_dim = queries.shape
    group_size = HEADS // KVH
    kv_here = max(1, heads_here // group_size)
    per_kv = heads_here // kv_here
    sharing = max(1, group_size // heads_here)
    peers = lax.axis_size("seq") - 1
    chunks = rows_here // ROWS
    width = PAD + rows_here
    pairs = per_kv // 2
    far = pl.BlockSpec(memory_space=pl.ANY)
    whole = pl.BlockSpec(memory_space=pltpu.VMEM)
    flat = jax.ShapeDtypeStruct((rows_here * heads_here, head_dim), jnp.bfloat16)
    f32, bf16 = jnp.float32, jnp.bfloat16
    attention, query_gradient, own, arrived = pl.pallas_call(
        functools.partial(
            attend, heads_here, kv_here, per_kv, chunks, peers, sharing == 1, 1.0 / math.sqrt(head_dim)
        ),
        in_specs=[pl.BlockSpec(memory_space=pltpu.SMEM)] * 2 + [far, far, far, whole],
        out_specs=[whole] * 4,
        out_shape=[
            flat,
            flat,
            jax.ShapeDtypeStruct((rows_here, kv_here * 2 * head_dim), bf16),
            jax.ShapeDtypeStruct((PMAX, kv_here * 2 * head_dim), bf16),
        ],
        scratch_shapes=[pltpu.VMEM((rows_here * heads_here, head_dim), bf16)] * 2
        + [pltpu.VMEM((rows_here * 2 * KVH, head_dim), bf16)]
        + [pltpu.VMEM((rows_here * heads_here, head_dim), f32)] * 3
        + [
            pltpu.VMEM((rows_here * max(heads_here, 2 * KVH), head_dim), f32),
            pltpu.VMEM((kv_here, width, head_dim), bf16),
            pltpu.VMEM((kv_here, width, 2 * head_dim), bf16),
            pltpu.VMEM((rows_here, 128), f32),
            pltpu.VMEM((ROWS, width), f32),
            pltpu.VMEM((kv_here, head_dim, width), f32),
            pltpu.VMEM((kv_here, head_dim, width), f32),
            pltpu.VMEM((pairs, 2 * ROWS, chunks * (chunks + 1) // 2 * ROWS), f32),
            pltpu.VMEM((pairs, 2 * ROWS, chunks * (chunks + 1) // 2 * ROWS), f32),
            pltpu.VMEM((pairs, 2 * ROWS, width), bf16),
            pltpu.VMEM((pairs, 2 * ROWS, width), bf16),
            pltpu.VMEM((pairs, 2 * ROWS, head_dim), bf16),
            pltpu.VMEM((2 * kv_here * PMAX, head_dim), bf16),
            pltpu.VMEM((peers, 2 * kv_here * PMAX, head_dim), bf16),
            pltpu.VMEM((kv_here, PMAX, 2 * head_dim), bf16),
            pltpu.VMEM((kv_here, peers, PMAX, 2 * head_dim), bf16),
            pltpu.SemaphoreType.DMA((peers,)),
            pltpu.SemaphoreType.DMA((peers,)),
            pltpu.SemaphoreType.DMA((kv_here, peers)),
            pltpu.SemaphoreType.DMA((kv_here, peers)),
            pltpu.SemaphoreType.DMA((2,)),
            pltpu.SemaphoreType.DMA((chunks,)),
            pltpu.SemaphoreType.DMA((chunks,)),
        ],
        compiler_params=pltpu.CompilerParams(
            vmem_limit_bytes=48 * 2**20, collective_id=0, has_side_effects=True
        ),
    )(
        partner,
        prompt_blocks,
        queries.reshape(-1, head_dim),
        grad_out.reshape(-1, head_dim),
        keys_values.reshape(-1, head_dim),
        segments.reshape(1, rows_here),
    )
    if sharing > 1:
        joined = lax.optimization_barrier(jnp.concatenate([own, arrived], axis=0))
        summed = head_total(joined.astype(jnp.float32), sharing)
        own, arrived = summed[:rows_here], summed[rows_here:].astype(jnp.bfloat16)
        head_rows = own[:PMAX] + arrived.astype(jnp.float32)
        own = jnp.concatenate([head_rows, own[PMAX:]], axis=0).astype(jnp.bfloat16)
    return (attention.reshape(queries.shape), query_gradient.reshape(queries.shape), own)


def solution(mesh):
    in_specs = (
        P("seq", "head", None),
        P("seq", None, None, None),
        P("seq", "head", None),
        P("seq"),
        P(),
        P(),
    )
    out_specs = (P("seq", "head", None), P("seq", "head", None), P("seq", "head"))
    return jax.shard_map(body, mesh=mesh, in_specs=in_specs, out_specs=out_specs, check_vma=False)
```

```python
import functools
import math

import jax
import jax.numpy as jnp
from jax import lax
from jax.experimental import pallas as pl
from jax.experimental.pallas import tpu as pltpu
from jax.sharding import PartitionSpec as P

HEADS = 64
KVH = 8
PMAX = 64
BLK = 16
ROWS = 128
PAD = 128
TILE = 32
TOGETHER = 4
MASKED = -1e30
LOG2E = math.log2(math.e)


def from_partner(value, axis, apart):
    mask = 2**apart
    pairs = [(source, source ^ mask) for source in range(lax.axis_size(axis))]
    return lax.ppermute(value, axis, pairs)


def head_total(block, sharing):
    flat = block.reshape(block.shape[0], -1)
    place = lax.axis_index("head")
    for bit in reversed(range(sharing.bit_length() - 1)):
        half = flat.shape[1] // 2
        mine = place // 2**bit % 2
        kept = lax.dynamic_slice_in_dim(flat, mine * half, half, 1)
        given = lax.dynamic_slice_in_dim(flat, (1 - mine) * half, half, 1)
        got = from_partner(given.astype(jnp.bfloat16), "head", bit).astype(given.dtype)
        flat = kept + got
    return flat


def dot(a, b):
    return jnp.dot(a, b, preferred_element_type=jnp.float32)


def dot_t(a, b):
    return lax.dot_general(a, b, (((1,), (1,)), ((), ())), preferred_element_type=jnp.float32)


def attend(
    heads, kvs, per_kv, chunks, peers, merge, scale,
    partner_ref, blocks_ref, q_hbm, do_hbm, kv_hbm, seg_ref,
    out_ref, dq_ref, own_ref, arrived_ref,
    q_ref, do_ref, kv_ref,
    qf, dof, dqf, af, kcat, vcat, segc, bias, dkt, dvt,
    early_s, early_dp, kept_pb, kept_ds, kept_dos,
    parcel, got, grads, got_grads, sent, landed, grads_sent, grads_landed, kv_sem, q_sem, do_sem,
):
    me = lax.axis_index("seq")
    kvf = af
    rows = chunks * ROWS
    width = PAD + rows
    piece = ROWS * heads
    last = chunks - 1

    def prompt_copy(d):
        return pltpu.make_async_remote_copy(
            src_ref=parcel,
            dst_ref=got.at[d],
            send_sem=sent.at[d],
            recv_sem=landed.at[d],
            device_id={"seq": lax.rem(me + d + 1, peers + 1)},
            device_id_type=pl.DeviceIdType.MESH,
        )

    def grad_copy(g, d):
        return pltpu.make_async_remote_copy(
            src_ref=grads.at[g],
            dst_ref=got_grads.at[g, d],
            send_sem=grads_sent.at[g, d],
            recv_sem=grads_landed.at[g, d],
            device_id={"seq": lax.rem(me + d + 1, peers + 1)},
            device_id_type=pl.DeviceIdType.MESH,
        )

    def each_peer(act):
        def one(d, carry):
            act(d)
            return carry
        lax.fori_loop(0, peers, one, 0)

    def separately(act):
        pl.when(me >= 0)(act)

    def span(c):
        return pl.ds(c * piece, piece)

    early = PMAX * 2 * KVH
    loads = [
        pltpu.make_async_copy(kv_hbm.at[pl.ds(0, early)], kv_ref.at[pl.ds(0, early)], kv_sem.at[0]),
        pltpu.make_async_copy(
            kv_hbm.at[pl.ds(early, rows * 2 * KVH - early)],
            kv_ref.at[pl.ds(early, rows * 2 * KVH - early)],
            kv_sem.at[1],
        ),
    ]
    q_loads = [pltpu.make_async_copy(q_hbm.at[span(c)], q_ref.at[span(c)], q_sem.at[c]) for c in range(chunks)]
    do_loads = [pltpu.make_async_copy(do_hbm.at[span(c)], do_ref.at[span(c)], do_sem.at[c]) for c in range(chunks)]
    for load in loads + q_loads + do_loads:
        load.start()
    barrier = pltpu.get_barrier_semaphore()
    each_peer(lambda d: pl.semaphore_signal(
        barrier, inc=1, device_id={"seq": lax.rem(me + d + 1, peers + 1)},
        device_id_type=pl.DeviceIdType.MESH,
    ))
    kv_start = lax.axis_index("head") * heads // (HEADS // KVH)
    loads[0].wait()
    kvf[:early, :] = kv_ref[:early, :].astype(jnp.float32)
    for n in range(2 * kvs):
        at = kv_start + n % kvs + n // kvs * KVH
        parcel[n * PMAX:(n + 1) * PMAX, :] = kvf[pl.ds(at, PMAX, stride=2 * KVH), :].astype(jnp.bfloat16)
    pl.semaphore_wait(barrier, peers)
    each_peer(lambda d: prompt_copy(d).start())
    loads[1].wait()
    kvf[early:, :] = kv_ref[early:, :].astype(jnp.float32)
    for g in range(kvs):
        k_rows = kvf[pl.ds(kv_start + g, rows, stride=2 * KVH), :]
        v_rows = kvf[pl.ds(kv_start + g + KVH, rows, stride=2 * KVH), :]
        kcat[g, PAD:, :] = k_rows.astype(jnp.bfloat16)
        vcat[g, PAD:, :128] = v_rows.astype(jnp.bfloat16)
        kcat[g, PMAX:PAD, :] = jnp.zeros((PAD - PMAX, 128), jnp.bfloat16)
        vcat[g, PMAX:PAD, :128] = jnp.zeros((PAD - PMAX, 128), jnp.bfloat16)
        vcat[g, :, 128:] = jnp.ones((width, 128), jnp.bfloat16)
    segc[...] = jnp.broadcast_to(seg_ref[...].astype(jnp.float32), (128, rows)).T
    dkt[...] = jnp.zeros_like(dkt)
    dvt[...] = jnp.zeros_like(dvt)

    pairs = per_kv // TOGETHER

    def spots(g, c, i):
        h = g * per_kv + TOGETHER * i + c * piece
        return [pl.ds(h + n, ROWS, stride=heads) for n in range(TOGETHER)]

    def both(ref, g, c, i):
        return jnp.concatenate([ref[spot, :] for spot in spots(g, c, i)], axis=0)

    def prepare(c):
        q_loads[c].wait()
        do_loads[c].wait()
        qf[span(c), :] = q_ref[span(c), :].astype(jnp.float32)
        dof[span(c), :] = do_ref[span(c), :].astype(jnp.float32)
        size = (c + 1) * ROWS
        start = c * (c + 1) // 2 * ROWS
        for i in range(pairs):
            q = both(qf, 0, c, i).astype(jnp.bfloat16)
            do = both(dof, 0, c, i).astype(jnp.bfloat16)
            early_s[i, :, start:start + size] = dot_t(q, kcat[0, PAD:PAD + size, :])
            early_dp[i, :, start:start + size] = dot_t(do, vcat[0, PAD:PAD + size, :128])

    for c in range(chunks):
        separately(functools.partial(prepare, c))

    each_peer(lambda d: prompt_copy(d).wait())
    slot = jnp.maximum(lax.rem(me - partner_ref[me] + peers + 1, peers + 1) - 1, 0)
    for g in range(kvs):
        kcat[g, :PMAX, :] = got[slot, g * PMAX:(g + 1) * PMAX, :]
        vcat[g, :PMAX, :128] = got[slot, (kvs + g) * PMAX:(kvs + g + 1) * PMAX, :]

    def work(g, c):
        wide = PAD + (c + 1) * ROWS
        size = (c + 1) * ROWS
        start = c * (c + 1) // 2 * ROWS
        final = g == kvs - 1 and c == last
        live = BLK * blocks_ref[partner_ref[me]]
        column = segc[c * ROWS:(c + 1) * ROWS, :]
        place = lax.broadcasted_iota(jnp.int32, (ROWS, 128), 1)
        row = lax.broadcasted_iota(jnp.int32, (ROWS, 128), 0)
        bias[:, :PAD] = jnp.where((column == 1.0) & (place < live), 0.0, MASKED)
        for j in range(c + 1):
            same = column == seg_ref[:, j * ROWS:(j + 1) * ROWS].astype(jnp.float32)
            if j == c:
                same = same & (place <= row)
            bias[:, PAD + j * ROWS:PAD + (j + 1) * ROWS] = jnp.where(same, 0.0, MASKED)

        def scores(i):
            q = both(qf, g, c, i).astype(jnp.bfloat16)
            do = both(dof, g, c, i)
            low = do.astype(jnp.bfloat16)
            if g == 0:
                s = jnp.concatenate([dot_t(q, kcat[g, :PAD, :]), early_s[i, :, start:start + size]], axis=1)
                dp = jnp.concatenate([dot_t(low, vcat[g, :PAD, :128]), early_dp[i, :, start:start + size]], axis=1)
            else:
                s = dot_t(q, kcat[g, :wide, :])
                dp = dot_t(low, vcat[g, :wide, :128])
            return q, do, s, dp

        def softmax(i, q, do, s, dp):
            tiles = [slice(r, r + TILE) for r in range(0, TOGETHER * ROWS, TILE)]
            low = []
            for tile in tiles:
                row = tile.start % ROWS
                t = s[tile] * (scale * LOG2E) + bias[row:row + TILE, :wide]
                low.append(jnp.exp2(t - jnp.max(t, axis=1, keepdims=True)).astype(jnp.bfloat16))
            pb = jnp.concatenate(low, axis=0)
            mixed = dot(pb, vcat[g, :wide, :])
            outs, doss, dss = [], [], []
            for tile, p in zip(tiles, low):
                inverse = 1.0 / mixed[tile, 128:]
                attention = (mixed[tile, :128] * inverse).astype(jnp.bfloat16).astype(jnp.float32)
                outs.append(attention)
                doss.append((do[tile] * inverse).astype(jnp.bfloat16))
                delta = jnp.sum(do[tile] * attention, axis=1, keepdims=True)
                dss.append(p * ((dp[tile] - delta) * inverse[:, :1]).astype(jnp.bfloat16))
            attention = jnp.concatenate(outs, axis=0)
            for n, spot in enumerate(spots(g, c, i)):
                af[spot, :] = attention[n * ROWS:(n + 1) * ROWS]
            return q, pb, jnp.concatenate(doss, axis=0), jnp.concatenate(dss, axis=0)

        def query_part(i, ds):
            dq = dot(ds, kcat[g, :wide, :]) * scale
            for n, spot in enumerate(spots(g, c, i)):
                dqf[spot, :] = dq[n * ROWS:(n + 1) * ROWS]

        def gradients(i, q, pb, dos, ds):
            if final:
                kept_pb[i], kept_ds[i], kept_dos[i] = pb, ds, dos
                dkt[g, :, :PAD] += dot(q.T, ds[:, :PAD])
                dvt[g, :, :PAD] += dot(dos.T, pb[:, :PAD])
            else:
                query_part(i, ds)
                dkt[g, :, :wide] += dot(q.T, ds)
                dvt[g, :, :wide] += dot(dos.T, pb)

        scored, soft = {}, {}
        for i in range(pairs + 2):
            if i < pairs:
                scored[i] = scores(i)
            if 0 <= i - 1 < pairs:
                soft[i - 1] = softmax(i - 1, *scored.pop(i - 1))
            if 0 <= i - 2 < pairs:
                gradients(i - 2, *soft.pop(i - 2))
        if c == last:
            for part, total in ((0, dkt), (1, dvt)):
                grads[g, :, part * 128:(part + 1) * 128] = (
                    (total[g, :, :PAD] * (1.0 if part else scale)).T[:PMAX].astype(jnp.bfloat16)
                )
            each_peer(lambda d: grad_copy(g, d).start())
        if final:
            for i in range(pairs):
                q = both(qf, g, c, i).astype(jnp.bfloat16)
                ds, pb, dos = kept_ds[i], kept_pb[i], kept_dos[i]
                query_part(i, ds)
                dkt[g, :, PAD:] += dot(q.T, ds[:, PAD:])
                dvt[g, :, PAD:] += dot(dos.T, pb[:, PAD:])
        if c == last:
            for part, total in ((0, dkt), (1, dvt)):
                at = (2 * g + part) * 128
                own_ref[:, at:at + 128] = (
                    (total[g, :, PAD:] * (1.0 if part else scale)).T.astype(jnp.bfloat16)
                )
        if g == kvs - 1:
            out_ref[span(c), :] = af[span(c), :].astype(jnp.bfloat16)
            dq_ref[span(c), :] = dqf[span(c), :].astype(jnp.bfloat16)

    for g in range(kvs):
        for c in range(chunks):
            separately(functools.partial(work, g, c))

    slot = jnp.int32(0)
    for b in range(peers + 1):
        slot = jnp.where(partner_ref[b] == me, lax.rem(me - b + peers + 1, peers + 1) - 1, slot)
    slot = jnp.maximum(slot, 0)
    for g in range(kvs):
        each_peer(lambda d: grad_copy(g, d).wait())
    for g in range(kvs):
        block = got_grads[g, slot]
        at = slice(g * 256, (g + 1) * 256)
        arrived_ref[:, at] = block
        if merge:
            own_ref[:PMAX, at] = (
                own_ref[:PMAX, at].astype(jnp.float32) + block.astype(jnp.float32)
            ).astype(jnp.bfloat16)


def body(queries, keys_values, grad_out, segments, partner, prompt_blocks):
    rows_here, heads_here, head_dim = queries.shape
    group_size = HEADS // KVH
    kv_here = max(1, heads_here // group_size)
    per_kv = heads_here // kv_here
    sharing = max(1, group_size // heads_here)
    peers = lax.axis_size("seq") - 1
    chunks = rows_here // ROWS
    width = PAD + rows_here
    pairs = per_kv // TOGETHER
    far = pl.BlockSpec(memory_space=pl.ANY)
    whole = pl.BlockSpec(memory_space=pltpu.VMEM)
    flat = jax.ShapeDtypeStruct((rows_here * heads_here, head_dim), jnp.bfloat16)
    f32, bf16 = jnp.float32, jnp.bfloat16
    attention, query_gradient, own, arrived = pl.pallas_call(
        functools.partial(
            attend, heads_here, kv_here, per_kv, chunks, peers, sharing == 1, 1.0 / math.sqrt(head_dim)
        ),
        in_specs=[pl.BlockSpec(memory_space=pltpu.SMEM)] * 2 + [far, far, far, whole],
        out_specs=[whole] * 4,
        out_shape=[
            flat,
            flat,
            jax.ShapeDtypeStruct((rows_here, kv_here * 2 * head_dim), bf16),
            jax.ShapeDtypeStruct((PMAX, kv_here * 2 * head_dim), bf16),
        ],
        scratch_shapes=[pltpu.VMEM((rows_here * heads_here, head_dim), bf16)] * 2
        + [pltpu.VMEM((rows_here * 2 * KVH, head_dim), bf16)]
        + [pltpu.VMEM((rows_here * heads_here, head_dim), f32)] * 3
        + [
            pltpu.VMEM((rows_here * max(heads_here, 2 * KVH), head_dim), f32),
            pltpu.VMEM((kv_here, width, head_dim), bf16),
            pltpu.VMEM((kv_here, width, 2 * head_dim), bf16),
            pltpu.VMEM((rows_here, 128), f32),
            pltpu.VMEM((ROWS, width), f32),
            pltpu.VMEM((kv_here, head_dim, width), f32),
            pltpu.VMEM((kv_here, head_dim, width), f32),
            pltpu.VMEM((pairs, TOGETHER * ROWS, chunks * (chunks + 1) // 2 * ROWS), f32),
            pltpu.VMEM((pairs, TOGETHER * ROWS, chunks * (chunks + 1) // 2 * ROWS), f32),
            pltpu.VMEM((pairs, TOGETHER * ROWS, width), bf16),
            pltpu.VMEM((pairs, TOGETHER * ROWS, width), bf16),
            pltpu.VMEM((pairs, TOGETHER * ROWS, head_dim), bf16),
            pltpu.VMEM((2 * kv_here * PMAX, head_dim), bf16),
            pltpu.VMEM((peers, 2 * kv_here * PMAX, head_dim), bf16),
            pltpu.VMEM((kv_here, PMAX, 2 * head_dim), bf16),
            pltpu.VMEM((kv_here, peers, PMAX, 2 * head_dim), bf16),
            pltpu.SemaphoreType.DMA((peers,)),
            pltpu.SemaphoreType.DMA((peers,)),
            pltpu.SemaphoreType.DMA((kv_here, peers)),
            pltpu.SemaphoreType.DMA((kv_here, peers)),
            pltpu.SemaphoreType.DMA((2,)),
            pltpu.SemaphoreType.DMA((chunks,)),
            pltpu.SemaphoreType.DMA((chunks,)),
        ],
        compiler_params=pltpu.CompilerParams(
            vmem_limit_bytes=48 * 2**20, collective_id=0, has_side_effects=True
        ),
    )(
        partner,
        prompt_blocks,
        queries.reshape(-1, head_dim),
        grad_out.reshape(-1, head_dim),
        keys_values.reshape(-1, head_dim),
        segments.reshape(1, rows_here),
    )
    if sharing > 1:
        joined = lax.optimization_barrier(jnp.concatenate([own, arrived], axis=0))
        summed = head_total(joined.astype(jnp.float32), sharing)
        own, arrived = summed[:rows_here], summed[rows_here:].astype(jnp.bfloat16)
        head_rows = own[:PMAX] + arrived.astype(jnp.float32)
        own = jnp.concatenate([head_rows, own[PMAX:]], axis=0).astype(jnp.bfloat16)
    return (attention.reshape(queries.shape), query_gradient.reshape(queries.shape), own)


def solution(mesh):
    in_specs = (
        P("seq", "head", None),
        P("seq", None, None, None),
        P("seq", "head", None),
        P("seq"),
        P(),
        P(),
    )
    out_specs = (P("seq", "head", None), P("seq", "head", None), P("seq", "head"))
    return jax.shard_map(body, mesh=mesh, in_specs=in_specs, out_specs=out_specs, check_vma=False)
```
